32 devices in a mesh: dp: 16 (over z, y, core), grp: 2 (over x).
Axes of the slice: x: 2, y: 2, z: 4, core: 2. Of those that a mesh axis runs over, the one named last changes fastest.
Arguments:
- activations: bfloat16 [8192, 3072], P('dp', 'grp'), may hold values from -125 to 125
- cotangents: bfloat16 [8192, 3072], P('dp', 'grp'), may hold values from -125 to 125
Outputs:
- update: float32 [3072, 3072], P('dp', 'grp')
The draws below stay inside these ranges and needn't reach their ends.
All inputs are finite; a program needn't handle non-finite values.
Results may differ from the reference program's by a relative error of at most 0.009.
Values may be sent and summed in bfloat16 or wider, within the bound.
A program may use at most 192 MiB of HBM per device.

```python
import math
import jax
import jax.numpy as jnp
from jax import lax

D = 3072
R = 512
ITERS = 3
ROWS = 8192
N_DP = 16


def draw_scaled(key, stream_salt):
    base_key = jax.random.fold_in(key, stream_salt)
    values_key, column_key, row_key = jax.random.split(base_key, 3)
    rising = jnp.exp(math.log(3.0) * jnp.arange(D, dtype=jnp.float32) / D)
    column_scale = jnp.exp(jax.random.uniform(column_key, (D,), jnp.float32) * math.log(10.0)) * rising
    row_scale = jnp.exp(jax.random.uniform(row_key, (ROWS, 1), jnp.float32) * math.log(10.0))
    fluctuation = jax.random.truncated_normal(values_key, -4.0, 4.0, (ROWS, D), jnp.float32)
    return fluctuation * row_scale * column_scale / 10.0


def draw_activations(key, part):
    return draw_scaled(key, 11).astype(jnp.bfloat16)


def draw_cotangents(key, part):
    return draw_scaled(key, 23).astype(jnp.bfloat16)


def setup_inputs(seed: int = 0) -> dict:
    arg_keys = jax.random.split(jax.random.key(seed), 3)
    activations = draw_activations(jax.random.fold_in(arg_keys[2], 71), 0)
    cotangents = draw_cotangents(jax.random.fold_in(arg_keys[2], 71), 0)
    return {"activations": activations, "cotangents": cotangents}


damping = 0.05
epsilon = 1e-06

def block_terms(activations, cotangents, block_index):
    start_row = block_index * R
    inputs = lax.dynamic_slice_in_dim(activations, start_row, R, 0)
    grads = lax.dynamic_slice_in_dim(cotangents, start_row, R, 0)
    results = []
    for left_side, right_side in ((inputs, inputs), (grads, grads), (grads, inputs)):
        product = jnp.dot(left_side.T, right_side, preferred_element_type=jnp.float32)
        results.append(product)
    return results

def inverse_factor(covariance):
    identity = jnp.eye(D, dtype=jnp.float32)
    trace_sum = jnp.trace(covariance)
    damp_term = damping * trace_sum / D
    norm_square = jnp.sum(covariance * covariance) + 2.0 * damp_term * trace_sum + D * damp_term * damp_term
    scale_factor = lax.rsqrt(norm_square)
    base_matrix = (scale_factor * (covariance + damp_term * identity)).astype(jnp.bfloat16)
    iterate = (2.0 * identity - base_matrix.astype(jnp.float32)).astype(jnp.bfloat16)
    for sweep_index in range(ITERS - 1):
        product = jnp.dot(base_matrix, iterate, preferred_element_type=jnp.float32).astype(jnp.bfloat16)
        iterate = (2.0 * iterate.astype(jnp.float32) - jnp.dot(iterate, product, preferred_element_type=jnp.float32)).astype(jnp.bfloat16)
    return iterate

def reference(activations, cotangents):

    def add_block(totals, block_index):
        results = block_terms(activations, cotangents, block_index)
        return ((totals[0] + results[0], totals[1] + results[1], totals[2] + results[2]), None)
    zero_matrix = jnp.zeros((D, D), jnp.float32)
    sums, unused = lax.scan(add_block, (zero_matrix, zero_matrix, zero_matrix), jnp.arange(N_DP, dtype=jnp.int32))
    cov_inputs, cov_grads, gradient = sums
    inverse_inputs = inverse_factor(cov_inputs)
    inverse_grads = inverse_factor(cov_grads)
    left_side = jnp.dot(inverse_grads, gradient.astype(jnp.bfloat16), preferred_element_type=jnp.float32).astype(jnp.bfloat16)
    preconditioned = jnp.dot(left_side, inverse_inputs, preferred_element_type=jnp.float32)
    return preconditioned * lax.rsqrt(jnp.mean(preconditioned * preconditioned) + epsilon)
```

```python
import jax
import jax.numpy as jnp
from jax import lax
from jax.sharding import PartitionSpec as P

damping = 0.05
epsilon = 1e-06
f32 = jnp.float32
bf16 = jnp.bfloat16


def dot_rows(left, right):
    return lax.dot_general(left, right, (((0,), (0,)), ((), ())), preferred_element_type=f32)


def matmul(left, right):
    return jnp.dot(left, right, preferred_element_type=f32)


def shards(activations, cotangents):
    n = lax.axis_size("dp")
    c = lax.axis_size("grp")
    chips = n // 2
    part = c // 2
    cols = activations.shape[1]
    D = cols * c
    rows = D // n
    half = D // 2
    dp_index = lax.axis_index("dp")
    grp_index = lax.axis_index("grp")
    core = dp_index % 2
    on_g = grp_index >= part
    pairs = [(i, i ^ 1) for i in range(n)]
    same_core = [list(range(0, n, 2)), list(range(1, n, 2))]

    def other_core(x):
        return lax.ppermute(x, "dp", pairs)

    def core_halves(mine):
        theirs = other_core(mine)
        return jnp.where(
            core == 0,
            jnp.concatenate([mine, theirs], axis=0),
            jnp.concatenate([theirs, mine], axis=0),
        )

    def reduce_rows(x):
        return lax.psum_scatter(
            x, "dp", scatter_dimension=0, tiled=True, axis_index_groups=same_core
        )

    if c == 2:
        theirs = lax.ppermute(jnp.where(on_g, activations, cotangents), "grp", [(0, 1), (1, 0)])
        mine = jnp.where(
            on_g,
            jnp.concatenate([theirs, cotangents], axis=1),
            jnp.concatenate([activations, theirs], axis=1),
        )
    else:
        mine = jnp.where(
            on_g,
            lax.all_gather(cotangents, "grp", axis=1, tiled=True),
            lax.all_gather(activations, "grp", axis=1, tiled=True),
        )
    mine = jnp.concatenate([mine, other_core(mine)], axis=0)
    my_half = lax.dynamic_slice_in_dim(mine, core * half, half, 1)
    cov_rows = reduce_rows(dot_rows(my_half, mine).astype(bf16))

    all_grads = lax.all_gather(cotangents, "grp", axis=1, tiled=True)
    all_grads = jnp.concatenate([all_grads, other_core(all_grads)], axis=0)
    acts = jnp.concatenate([activations, other_core(activations)], axis=0)
    acts = lax.dynamic_slice_in_dim(acts, core * (cols // 2), cols // 2, 1)
    grad_rows = reduce_rows(dot_rows(acts, all_grads).astype(bf16))
    grad_rows = lax.all_gather(grad_rows, "grp", axis=0, tiled=True)

    cov = lax.all_gather(cov_rows, "dp", axis=0, tiled=True)
    cov = cov.reshape(chips, 2, rows, D).transpose(1, 0, 2, 3).reshape(D, D)
    wide = cov.astype(f32)
    diag = lax.iota(jnp.int32, D)[:, None] == lax.iota(jnp.int32, D)[None, :]
    trace = jnp.sum(jnp.where(diag, wide, 0.0))
    square = jnp.sum(wide * wide)
    damp = damping * trace / D
    scale = lax.rsqrt(square + 2.0 * damp * trace + D * damp * damp)
    base = (scale * (wide + jnp.where(diag, damp, 0.0))).astype(bf16)

    def my_rows(x):
        return lax.dynamic_slice_in_dim(x, core * half, half, 0)

    base_half = my_rows(base)
    base_wide = base_half.astype(f32)
    second_wide = 2.0 * base_wide - matmul(base_half, base)
    second_half = second_wide.astype(bf16)
    second = core_halves(second_half)
    second_wide = second_half.astype(f32)
    fourth_half = (2.0 * second_wide - matmul(second_half, second)).astype(bf16)
    fourth = core_halves(fourth_half)
    mixed_half = (2.0 * (base_wide + second_wide) - matmul(base_half, second)).astype(bf16)
    tail_half = (
        4.0 * fourth_half.astype(f32) + 2.0 * mixed_half.astype(f32) - matmul(mixed_half, fourth)
    ).astype(bf16)
    tail = core_halves(tail_half)

    left = (8.0 * grad_rows.astype(f32) - matmul(grad_rows, tail)).astype(bf16)
    left = lax.all_to_all(left, "dp", split_axis=1, concat_axis=0, tiled=True)
    left = lax.ppermute(left, "grp", [(part + j, j) for j in range(part)])
    left = left.reshape(chips, 2, c, D // c // n, rows).transpose(2, 1, 0, 3, 4).reshape(D, rows)
    precond = 8.0 * left.astype(f32).T - dot_rows(left, tail)

    keep = lax.dynamic_slice_in_dim(precond, (grp_index % part) * cols, cols, 1)
    send = lax.dynamic_slice_in_dim(precond, (grp_index % part + part) * cols, cols, 1)
    sent = lax.ppermute(send.astype(bf16), "grp", [(j, part + j) for j in range(part)])
    precond = jnp.where(on_g, sent.astype(f32), keep)
    total = lax.psum(jnp.sum(precond * precond), ("dp", "grp"))
    return precond * lax.rsqrt(total / (D * D) + epsilon)


def solution(mesh):
    spec = P("dp", "grp")
    return jax.shard_map(shards, mesh=mesh, in_specs=(spec, spec), out_specs=spec, check_vma=False)
```

```python
import jax
import jax.numpy as jnp
from jax import lax
from jax.sharding import PartitionSpec as P

damping = 0.05
epsilon = 1e-06
f32 = jnp.float32
bf16 = jnp.bfloat16


def dot_rows(left, right):
    return lax.dot_general(left, right, (((0,), (0,)), ((), ())), preferred_element_type=f32)


def matmul(left, right):
    return jnp.dot(left, right, preferred_element_type=f32)


def shards(activations, cotangents):
    n = lax.axis_size("dp")
    c = lax.axis_size("grp")
    chips = n // 2
    part = c // 2
    cols = activations.shape[1]
    D = cols * c
    rows = D // n
    half = D // 2
    dp_index = lax.axis_index("dp")
    grp_index = lax.axis_index("grp")
    core = dp_index % 2
    on_g = grp_index >= part
    pairs = [(i, i ^ 1) for i in range(n)]
    same_core = [list(range(0, n, 2)), list(range(1, n, 2))]

    def other_core(x):
        return lax.ppermute(x, "dp", pairs)

    def core_halves(mine):
        theirs = other_core(mine)
        return jnp.where(
            core == 0,
            jnp.concatenate([mine, theirs], axis=0),
            jnp.concatenate([theirs, mine], axis=0),
        )

    def reduce_rows(x):
        return lax.psum_scatter(
            x, "dp", scatter_dimension=0, tiled=True, axis_index_groups=same_core
        )

    ring = list(range(0, chips, 2)) + list(range(chips - 1, 0, -2))
    chip = dp_index // 2
    place = jnp.where(chip % 2 == 0, chip // 2, chips - 1 - chip // 2)

    def ring_reduce(x, lanes):
        width = x.shape[1] // (2 * lanes)

        def block(lane, spot):
            spot = (spot + 2 * chips) % chips
            owner = jnp.where(spot < chips // 2, 2 * spot, 2 * (chips - 1 - spot) + 1)
            piece = lax.dynamic_slice(x, (owner * rows, lane * width), (rows, width))
            return piece.astype(f32)

        totals = [None] * (2 * lanes)
        for lane in range(2 * lanes):
            totals[lane] = block(lane, place + (1 if lane % 2 else -1))
        for step in range(chips - 1):
            for lane in range(2 * lanes):
                way = -1 if lane % 2 else 1
                moves = [
                    (ring[p] * 2 + k, ring[(p + way) % chips] * 2 + k)
                    for p in range(chips)
                    for k in range(2)
                ]
                got = lax.ppermute(totals[lane].astype(bf16), "dp", moves)
                totals[lane] = got.astype(f32) + block(lane, place - way * (step + 2))
        return jnp.concatenate(totals, axis=1)

    def sum_dp(x):
        hop = 1
        while hop < n:
            x = x + lax.ppermute(x, "dp", [(i, i ^ hop) for i in range(n)])
            hop *= 2
        return x

    if c == 2:
        theirs = lax.ppermute(jnp.where(on_g, activations, cotangents), "grp", [(0, 1), (1, 0)])
        mine = jnp.where(
            on_g,
            jnp.concatenate([theirs, cotangents], axis=1),
            jnp.concatenate([activations, theirs], axis=1),
        )
    else:
        all_grads = lax.all_gather(cotangents, "grp", axis=1, tiled=True)
        mine = jnp.where(
            on_g, all_grads, lax.all_gather(activations, "grp", axis=1, tiled=True)
        )
    mine = jnp.concatenate([mine, other_core(mine)], axis=0)
    my_half = lax.dynamic_index_in_dim(
        mine.reshape(mine.shape[0], chips, 2, rows), core, 2, keepdims=False
    ).reshape(mine.shape[0], half)
    cov_rows = ring_reduce(dot_rows(my_half, mine).astype(bf16), 2)

    if c == 2:
        rest = lax.ppermute(cotangents, "grp", [(1, 0)])
        all_grads = jnp.concatenate([cotangents, rest], axis=1)
    all_grads = jnp.concatenate([all_grads, other_core(all_grads)], axis=0)
    if c == 2:
        all_grads = jnp.where(on_g, mine, all_grads)
    acts = jnp.concatenate([activations, other_core(activations)], axis=0)
    acts = lax.dynamic_slice_in_dim(acts, core * (cols // 2), cols // 2, 1)
    grad_rows = reduce_rows(dot_rows(acts, all_grads).astype(bf16))
    if c == 2:
        first = lax.ppermute(grad_rows, "grp", [(0, 1)])
        grad_rows = jnp.concatenate([first, grad_rows], axis=0)
    else:
        grad_rows = lax.all_gather(grad_rows, "grp", axis=0, tiled=True)

    cov = lax.all_gather(cov_rows.astype(bf16), "dp", axis=0, tiled=True)

    def diag_mask(start, count):
        return start + lax.iota(jnp.int32, count)[:, None] == lax.iota(jnp.int32, D)[None, :]

    trace_part = jnp.sum(jnp.where(diag_mask(dp_index * rows, rows), cov_rows, 0.0))
    trace, square = sum_dp(jnp.stack([trace_part, jnp.sum(cov_rows * cov_rows)]))
    damp = damping * trace / D
    scale = lax.rsqrt(square + 2.0 * damp * trace + D * damp * damp)

    def my_rows(x):
        return lax.dynamic_slice_in_dim(x, core * half, half, 0)

    cov_half = my_rows(cov)
    cov_wide = cov_half.astype(f32)
    damp_half = jnp.where(diag_mask(core * half, half), damp, 0.0)
    base_wide = scale * (cov_wide + damp_half)
    base_square = scale * scale * (
        matmul(cov_half, cov) + 2.0 * damp * cov_wide + damp * damp_half
    )
    second_half = (2.0 * base_wide - base_square).astype(bf16)
    second = core_halves(second_half)
    second_wide = second_half.astype(f32)
    fourth_half = (2.0 * second_wide - matmul(second_half, second)).astype(bf16)
    fourth = core_halves(fourth_half)
    mixed_half = (
        2.0 * (base_wide + second_wide)
        - scale * (matmul(cov_half, second) + damp * second_wide)
    ).astype(bf16)
    tail_half = (
        4.0 * fourth_half.astype(f32) + 2.0 * mixed_half.astype(f32) - matmul(mixed_half, fourth)
    ).astype(bf16)
    tail = core_halves(tail_half)

    left = (8.0 * grad_rows.astype(f32) - matmul(grad_rows, tail)).astype(bf16)
    left = lax.all_to_all(left, "dp", split_axis=1, concat_axis=0, tiled=True)
    left = lax.ppermute(left, "grp", [(part + j, j) for j in range(part)])
    left = left.reshape(chips, 2, c, D // c // n, rows).transpose(2, 1, 0, 3, 4).reshape(D, rows)
    precond = 8.0 * left.astype(f32).T - dot_rows(left, tail)

    total = sum_dp(jnp.sum(precond * precond))

    keep = lax.dynamic_slice_in_dim(precond, (grp_index % part) * cols, cols, 1)
    send = lax.dynamic_slice_in_dim(precond, (grp_index % part + part) * cols, cols, 1)
    sent = lax.ppermute(send.astype(bf16), "grp", [(j, part + j) for j in range(part)])
    precond = jnp.where(on_g, sent.astype(f32), keep)
    total = lax.ppermute(total, "grp", [(j, part + j) for j in range(part)]) + jnp.where(
        on_g, 0.0, total
    )
    return precond * lax.rsqrt(total / (D * D) + epsilon)


def solution(mesh):
    spec = P("dp", "grp")
    return jax.shard_map(shards, mesh=mesh, in_specs=(spec, spec), out_specs=spec, check_vma=False)
```

```python
import math

import jax
import jax.numpy as jnp
from jax import lax
from jax.experimental import pallas as pl
from jax.experimental.pallas import tpu as pltpu
from jax.sharding import PartitionSpec as P

ITERS = 3
damping = 0.05
epsilon = 1e-06
f32 = jnp.float32
bf16 = jnp.bfloat16


def dot_rows(left, right):
    return lax.dot_general(left, right, (((0,), (0,)), ((), ())), preferred_element_type=f32)


def series(start, cov, scale, damp):
    rows, D = start.shape
    width = math.gcd(D, 512)
    terms = 2**ITERS - 1

    def kernel(scalar_ref, start_ref, cov_ref, out_ref, narrow_ref):
        scale = scalar_ref[0]
        damp = scalar_ref[1]
        out_ref[...] = start_ref[...]

        @pl.loop(0, terms)
        def _(term):
            narrow_ref[...] = out_ref[...].astype(bf16)

            @pl.loop(0, D // width)
            def _(block):
                at = pl.ds(pl.multiple_of(block * width, width), width)
                product = jnp.dot(narrow_ref[...], cov_ref[:, at], preferred_element_type=f32)
                total = out_ref[:, at]
                out_ref[:, at] = start_ref[:, at] + total - scale * (product + damp * total)

    vmem = pl.BlockSpec(memory_space=pltpu.VMEM)
    return pl.pallas_call(
        kernel,
        out_shape=jax.ShapeDtypeStruct((rows, D), f32),
        in_specs=[pl.BlockSpec(memory_space=pltpu.SMEM), vmem, vmem],
        out_specs=vmem,
        scratch_shapes=[pltpu.VMEM((rows, D), bf16)],
        compiler_params=pltpu.CompilerParams(vmem_limit_bytes=D * D * 2 + 24 * 1024 * 1024),
        cost_estimate=pl.CostEstimate(
            flops=2 * terms * rows * D * D,
            bytes_accessed=2 * D * D + 8 * rows * D,
            transcendentals=0,
        ),
        name="series",
    )(jnp.stack([scale, damp]), start, cov)


def shards(activations, cotangents):
    n = lax.axis_size("dp")
    c = lax.axis_size("grp")
    chips = n // 2
    part = c // 2
    cols = activations.shape[1]
    D = cols * c
    rows = D // n
    half = D // 2
    dp_index = lax.axis_index("dp")
    grp_index = lax.axis_index("grp")
    core = dp_index % 2
    on_g = grp_index >= part
    pairs = [(i, i ^ 1) for i in range(n)]

    def other_core(x):
        return lax.ppermute(x, "dp", pairs)

    ring = list(range(0, chips, 2)) + list(range(chips - 1, 0, -2))
    chip = dp_index // 2
    place = jnp.where(chip % 2 == 0, chip // 2, chips - 1 - chip // 2)

    def ring_reduce(x, lanes):
        width = x.shape[1] // (2 * lanes)
        count = x.shape[0] // chips

        def block(lane, spot):
            spot = (spot + 2 * chips) % chips
            owner = jnp.where(spot < chips // 2, 2 * spot, 2 * (chips - 1 - spot) + 1)
            piece = lax.dynamic_slice(x, (owner * count, lane * width), (count, width))
            return piece.astype(f32)

        totals = [None] * (2 * lanes)
        for lane in range(2 * lanes):
            totals[lane] = block(lane, place + (1 if lane % 2 else -1))
        for step in range(chips - 1):
            for lane in range(2 * lanes):
                way = -1 if lane % 2 else 1
                moves = [
                    (ring[p] * 2 + k, ring[(p + way) % chips] * 2 + k)
                    for p in range(chips)
                    for k in range(2)
                ]
                got = lax.ppermute(totals[lane].astype(bf16), "dp", moves)
                totals[lane] = got.astype(f32) + block(lane, place - way * (step + 2))
        return jnp.concatenate(totals, axis=1)

    def sum_dp(x):
        hop = 1
        while hop < n:
            x = x + lax.ppermute(x, "dp", [(i, i ^ hop) for i in range(n)])
            hop *= 2
        return x

    if c == 2:
        theirs = lax.ppermute(jnp.where(on_g, activations, cotangents), "grp", [(0, 1), (1, 0)])
        mine = jnp.where(
            on_g,
            jnp.concatenate([theirs, cotangents], axis=1),
            jnp.concatenate([activations, theirs], axis=1),
        )
    else:
        all_grads = lax.all_gather(cotangents, "grp", axis=1, tiled=True)
        mine = jnp.where(
            on_g, all_grads, lax.all_gather(activations, "grp", axis=1, tiled=True)
        )
    mine = jnp.concatenate([mine, other_core(mine)], axis=0)
    my_half = lax.dynamic_index_in_dim(
        mine.reshape(mine.shape[0], chips, 2, rows), core, 2, keepdims=False
    ).reshape(mine.shape[0], half)
    cov_part, cotangents = lax.optimization_barrier(
        (dot_rows(my_half, mine).astype(bf16), cotangents)
    )
    cov_rows = ring_reduce(cov_part, 2)

    if c == 2:
        rest = lax.ppermute(cotangents, "grp", [(1, 0)])
        all_grads = jnp.concatenate([cotangents, rest], axis=1)
    all_grads = jnp.concatenate([all_grads, other_core(all_grads)], axis=0)
    if c == 2:
        all_grads = jnp.where(on_g, mine, all_grads)
    acts = jnp.concatenate([activations, other_core(activations)], axis=0)
    acts = lax.dynamic_slice_in_dim(acts, core * (cols // 2), cols // 2, 1)
    grad_rows = ring_reduce(dot_rows(acts, all_grads).astype(bf16), 1).astype(bf16)
    if c == 2:
        first = lax.ppermute(grad_rows, "grp", [(0, 1)])
        grad_rows = jnp.concatenate([first, grad_rows], axis=0)
    else:
        grad_rows = lax.all_gather(grad_rows, "grp", axis=0, tiled=True)

    cov = lax.all_gather(cov_rows.astype(bf16), "dp", axis=0, tiled=True)

    def diag_mask(start, count):
        return start + lax.iota(jnp.int32, count)[:, None] == lax.iota(jnp.int32, D)[None, :]

    trace_part = jnp.sum(jnp.where(diag_mask(dp_index * rows, rows), cov_rows, 0.0))
    trace, square = sum_dp(jnp.stack([trace_part, jnp.sum(cov_rows * cov_rows)]))
    damp = damping * trace / D
    scale = lax.rsqrt(square + 2.0 * damp * trace + D * damp * damp)

    left = series(grad_rows.astype(f32), cov, scale, damp).astype(bf16)
    left = lax.all_to_all(left, "dp", split_axis=1, concat_axis=0, tiled=True)
    left = lax.ppermute(left, "grp", [(part + j, j) for j in range(part)])
    left = left.reshape(chips, 2, c, D // c // n, rows).transpose(2, 1, 0, 3, 4).reshape(D, rows)
    precond = series(left.T.astype(f32), cov, scale, damp)

    total = sum_dp(jnp.sum(precond * precond))

    keep = lax.dynamic_slice_in_dim(precond, (grp_index % part) * cols, cols, 1)
    send = lax.dynamic_slice_in_dim(precond, (grp_index % part + part) * cols, cols, 1)
    sent = lax.ppermute(send.astype(bf16), "grp", [(j, part + j) for j in range(part)])
    precond = jnp.where(on_g, sent.astype(f32), keep)
    total = lax.ppermute(total, "grp", [(j, part + j) for j in range(part)]) + jnp.where(
        on_g, 0.0, total
    )
    return precond * lax.rsqrt(total / (D * D) + epsilon)


def solution(mesh):
    spec = P("dp", "grp")
    return jax.shard_map(shards, mesh=mesh, in_specs=(spec, spec), out_specs=spec, check_vma=False)
```

```python
import math

import jax
import jax.numpy as jnp
from jax import lax
from jax.experimental import pallas as pl
from jax.experimental.pallas import tpu as pltpu
from jax.sharding import PartitionSpec as P

ITERS = 3
damping = 0.05
epsilon = 1e-06
f32 = jnp.float32
bf16 = jnp.bfloat16


def dot_rows(left, right):
    return lax.dot_general(left, right, (((0,), (0,)), ((), ())), preferred_element_type=f32)


def series(start, cov, scale, damp):
    rows, D = start.shape
    width = math.gcd(D, 512)
    terms = 2**ITERS - 1

    def kernel(scalar_ref, start_ref, cov_ref, out_ref, narrow_ref):
        scale = scalar_ref[0]
        damp = scalar_ref[1]
        out_ref[...] = start_ref[...]

        @pl.loop(0, terms)
        def _(term):
            narrow_ref[...] = out_ref[...].astype(bf16)

            @pl.loop(0, D // width)
            def _(block):
                at = pl.ds(pl.multiple_of(block * width, width), width)
                product = jnp.dot(narrow_ref[...], cov_ref[:, at], preferred_element_type=f32)
                total = out_ref[:, at]
                out_ref[:, at] = start_ref[:, at] + total - scale * (product + damp * total)

    vmem = pl.BlockSpec(memory_space=pltpu.VMEM)
    return pl.pallas_call(
        kernel,
        out_shape=jax.ShapeDtypeStruct((rows, D), f32),
        in_specs=[pl.BlockSpec(memory_space=pltpu.SMEM), vmem, vmem],
        out_specs=vmem,
        scratch_shapes=[pltpu.VMEM((rows, D), bf16)],
        compiler_params=pltpu.CompilerParams(vmem_limit_bytes=D * D * 2 + 24 * 1024 * 1024),
        cost_estimate=pl.CostEstimate(
            flops=2 * terms * rows * D * D,
            bytes_accessed=2 * D * D + 8 * rows * D,
            transcendentals=0,
        ),
        name="series",
    )(jnp.stack([scale, damp]), start, cov)


def shards(activations, cotangents):
    n = lax.axis_size("dp")
    c = lax.axis_size("grp")
    chips = n // 2
    part = c // 2
    cols = activations.shape[1]
    D = cols * c
    rows = D // n
    half = D // 2
    dp_index = lax.axis_index("dp")
    grp_index = lax.axis_index("grp")
    core = dp_index % 2
    on_g = grp_index >= part
    pairs = [(i, i ^ 1) for i in range(n)]

    def other_core(x):
        return lax.ppermute(x, "dp", pairs)

    ring = list(range(0, chips, 2)) + list(range(chips - 1, 0, -2))
    chip = dp_index // 2
    place = jnp.where(chip % 2 == 0, chip // 2, chips - 1 - chip // 2)

    def ring_reduce(x, lanes, beside=()):
        width = x.shape[1] // (2 * lanes)
        count = x.shape[0] // chips

        def block(lane, spot):
            spot = (spot + 2 * chips) % chips
            owner = jnp.where(spot < chips // 2, 2 * spot, 2 * (chips - 1 - spot) + 1)
            piece = lax.dynamic_slice(x, (owner * count, lane * width), (count, width))
            return piece.astype(f32)

        made = None
        totals = [None] * (2 * lanes)
        for lane in range(2 * lanes):
            totals[lane] = block(lane, place + (1 if lane % 2 else -1))
        for step in range(chips - 1):
            for lane in range(2 * lanes):
                way = -1 if lane % 2 else 1
                moves = [
                    (ring[p] * 2 + k, ring[(p + way) % chips] * 2 + k)
                    for p in range(chips)
                    for k in range(2)
                ]
                got = lax.ppermute(totals[lane].astype(bf16), "dp", moves)
                totals[lane] = got.astype(f32) + block(lane, place - way * (step + 2))
            for due, make in beside:
                if due == step:
                    made = make(made)
                    totals, made = lax.optimization_barrier((totals, made))
        return jnp.concatenate(totals, axis=1), made

    def sum_dp(x):
        hop = 1
        while hop < n:
            x = x + lax.ppermute(x, "dp", [(i, i ^ hop) for i in range(n)])
            hop *= 2
        return x

    if c == 2:
        theirs = lax.ppermute(jnp.where(on_g, activations, cotangents), "grp", [(0, 1), (1, 0)])
        mine = jnp.where(
            on_g,
            jnp.concatenate([theirs, cotangents], axis=1),
            jnp.concatenate([activations, theirs], axis=1),
        )
    else:
        all_grads = lax.all_gather(cotangents, "grp", axis=1, tiled=True)
        mine = jnp.where(
            on_g, all_grads, lax.all_gather(activations, "grp", axis=1, tiled=True)
        )
    mine = jnp.concatenate([mine, other_core(mine)], axis=0)
    my_half = lax.dynamic_index_in_dim(
        mine.reshape(mine.shape[0], chips, 2, rows), core, 2, keepdims=False
    ).reshape(mine.shape[0], half)
    cov_part, cotangents = lax.optimization_barrier(
        (dot_rows(my_half, mine).astype(bf16), cotangents)
    )

    def fetch_grads(unused):
        if c == 2:
            return lax.ppermute(cotangents, "grp", [(1, 0)])
        return all_grads

    def share_grads(fetched):
        if c == 2:
            fetched = jnp.concatenate([cotangents, fetched], axis=1)
        return fetched, other_core(fetched)

    def grad_product(shared):
        whole = jnp.concatenate(shared, axis=0)
        if c == 2:
            whole = jnp.where(on_g, mine, whole)
        acts = jnp.concatenate([activations, other_core(activations)], axis=0)
        acts = lax.dynamic_slice_in_dim(acts, core * (cols // 2), cols // 2, 1)
        return dot_rows(acts, whole).astype(bf16)

    cov_rows, grad_part = ring_reduce(
        cov_part,
        2,
        ((chips // 2 - 1, fetch_grads), (chips - 4, share_grads), (chips - 3, grad_product)),
    )

    cov = lax.all_gather(cov_rows.astype(bf16), "dp", axis=0, tiled=True)

    def diag_mask(start, count):
        return start + lax.iota(jnp.int32, count)[:, None] == lax.iota(jnp.int32, D)[None, :]

    trace_part = jnp.sum(jnp.where(diag_mask(dp_index * rows, rows), cov_rows, 0.0))
    parts = jnp.stack([trace_part, jnp.sum(cov_rows * cov_rows)])
    grad_rows, sums = ring_reduce(grad_part, 1, ((chips - 3, lambda unused: sum_dp(parts)),))
    grad_rows = grad_rows.astype(bf16)
    if c == 2:
        first = lax.ppermute(grad_rows, "grp", [(0, 1)])
        grad_rows = jnp.concatenate([first, grad_rows], axis=0)
    else:
        grad_rows = lax.all_gather(grad_rows, "grp", axis=0, tiled=True)
    trace, square = sums
    damp = damping * trace / D
    scale = lax.rsqrt(square + 2.0 * damp * trace + D * damp * damp)

    left = series(grad_rows.astype(f32), cov, scale, damp).astype(bf16)
    left = lax.all_to_all(left, "dp", split_axis=1, concat_axis=0, tiled=True)
    left = lax.ppermute(left, "grp", [(part + j, j) for j in range(part)])
    left = left.reshape(chips, 2, c, D // c // n, rows).transpose(2, 1, 0, 3, 4).reshape(D, rows)
    precond = series(left.T.astype(f32), cov, scale, damp)

    total = sum_dp(jnp.sum(precond * precond))

    keep = lax.dynamic_slice_in_dim(precond, (grp_index % part) * cols, cols, 1)
    send = lax.dynamic_slice_in_dim(precond, (grp_index % part + part) * cols, cols, 1)
    sent = lax.ppermute(send.astype(bf16), "grp", [(j, part + j) for j in range(part)])
    precond = jnp.where(on_g, sent.astype(f32), keep)
    total = lax.ppermute(total, "grp", [(j, part + j) for j in range(part)]) + jnp.where(
        on_g, 0.0, total
    )
    return precond * lax.rsqrt(total / (D * D) + epsilon)


def solution(mesh):
    spec = P("dp", "grp")
    return jax.shard_map(shards, mesh=mesh, in_specs=(spec, spec), out_specs=spec, check_vma=False)
```

```python
import math

import jax
import jax.numpy as jnp
from jax import lax
from jax.experimental import pallas as pl
from jax.experimental.pallas import tpu as pltpu
from jax.sharding import PartitionSpec as P

ITERS = 3
damping = 0.05
epsilon = 1e-06
f32 = jnp.float32
bf16 = jnp.bfloat16


def dot_rows(left, right):
    return lax.dot_general(left, right, (((0,), (0,)), ((), ())), preferred_element_type=f32)


def series(start, cov, scale, damp):
    rows, D = start.shape
    width = math.gcd(D, 512)
    terms = 2**ITERS - 1

    def kernel(scalar_ref, start_ref, cov_ref, out_ref, narrow_ref):
        scale = scalar_ref[0]
        damp = scalar_ref[1]
        out_ref[...] = start_ref[...]

        @pl.loop(0, terms)
        def _(term):
            narrow_ref[...] = out_ref[...].astype(bf16)

            @pl.loop(0, D // width)
            def _(block):
                at = pl.ds(pl.multiple_of(block * width, width), width)
                product = jnp.dot(narrow_ref[...], cov_ref[:, at], preferred_element_type=f32)
                total = out_ref[:, at]
                out_ref[:, at] = start_ref[:, at] + total - scale * (product + damp * total)

    vmem = pl.BlockSpec(memory_space=pltpu.VMEM)
    return pl.pallas_call(
        kernel,
        out_shape=jax.ShapeDtypeStruct((rows, D), f32),
        in_specs=[pl.BlockSpec(memory_space=pltpu.SMEM), vmem, vmem],
        out_specs=vmem,
        scratch_shapes=[pltpu.VMEM((rows, D), bf16)],
        compiler_params=pltpu.CompilerParams(vmem_limit_bytes=D * D * 2 + 24 * 1024 * 1024),
        cost_estimate=pl.CostEstimate(
            flops=2 * terms * rows * D * D,
            bytes_accessed=2 * D * D + 8 * rows * D,
            transcendentals=0,
        ),
        name="series",
    )(jnp.stack([scale, damp]), start, cov)


def shards(activations, cotangents):
    n = lax.axis_size("dp")
    c = lax.axis_size("grp")
    chips = n // 2
    part = c // 2
    cols = activations.shape[1]
    D = cols * c
    rows = D // n
    half = D // 2
    dp_index = lax.axis_index("dp")
    grp_index = lax.axis_index("grp")
    core = dp_index % 2
    on_g = grp_index >= part
    pairs = [(i, i ^ 1) for i in range(n)]

    def other_core(x):
        return lax.ppermute(x, "dp", pairs)

    ring = list(range(0, chips, 2)) + list(range(chips - 1, 0, -2))
    chip = dp_index // 2
    place = jnp.where(chip % 2 == 0, chip // 2, chips - 1 - chip // 2)

    def ring_reduce(x, lanes, beside=()):
        width = x.shape[1] // (2 * lanes)
        count = x.shape[0] // chips

        def block(lane, spot):
            spot = (spot + 2 * chips) % chips
            owner = jnp.where(spot < chips // 2, 2 * spot, 2 * (chips - 1 - spot) + 1)
            piece = lax.dynamic_slice(x, (owner * count, lane * width), (count, width))
            return piece.astype(f32)

        made = None
        totals = [None] * (2 * lanes)
        for lane in range(2 * lanes):
            totals[lane] = block(lane, place + (1 if lane % 2 else -1))
        for step in range(chips - 1):
            for lane in range(2 * lanes):
                way = -1 if lane % 2 else 1
                moves = [
                    (ring[p] * 2 + k, ring[(p + way) % chips] * 2 + k)
                    for p in range(chips)
                    for k in range(2)
                ]
                got = lax.ppermute(totals[lane].astype(bf16), "dp", moves)
                totals[lane] = got.astype(f32) + block(lane, place - way * (step + 2))
            for due, make in beside:
                if due == step:
                    made = make(made)
                    totals, made = lax.optimization_barrier((totals, made))
        return jnp.concatenate(totals, axis=1), made

    def sum_dp(x):
        hop = 1
        while hop < n:
            x = x + lax.ppermute(x, "dp", [(i, i ^ hop) for i in range(n)])
            hop *= 2
        return x

    if c == 2:
        theirs = lax.ppermute(jnp.where(on_g, activations, cotangents), "grp", [(0, 1), (1, 0)])
        mine = jnp.where(
            on_g,
            jnp.concatenate([theirs, cotangents], axis=1),
            jnp.concatenate([activations, theirs], axis=1),
        )
    else:
        all_grads = lax.all_gather(cotangents, "grp", axis=1, tiled=True)
        mine = jnp.where(
            on_g, all_grads, lax.all_gather(activations, "grp", axis=1, tiled=True)
        )
    mine = jnp.concatenate([mine, other_core(mine)], axis=0)
    my_half = lax.dynamic_index_in_dim(
        mine.reshape(mine.shape[0], chips, 2, rows), core, 2, keepdims=False
    ).reshape(mine.shape[0], half)
    cov_part, cotangents = lax.optimization_barrier(
        (dot_rows(my_half, mine).astype(bf16), cotangents)
    )

    def fetch_grads(unused):
        if c == 2:
            return lax.ppermute(cotangents, "grp", [(1, 0)])
        return all_grads

    def share_grads(fetched):
        if c == 2:
            fetched = jnp.concatenate([cotangents, fetched], axis=1)
        return fetched, other_core(fetched)

    def grad_product(shared):
        whole = jnp.concatenate(shared, axis=0)
        if c == 2:
            whole = jnp.where(on_g, mine, whole)
        acts = jnp.concatenate([activations, other_core(activations)], axis=0)
        acts = lax.dynamic_slice_in_dim(acts, core * (cols // 2), cols // 2, 1)
        return dot_rows(acts, whole).astype(bf16)

    cov_rows, grad_part = ring_reduce(
        cov_part,
        2,
        ((chips // 2 - 1, fetch_grads), (chips - 4, share_grads), (chips - 3, grad_product)),
    )

    cov = lax.all_gather(cov_rows.astype(bf16), "dp", axis=0, tiled=True)

    def diag_mask(start, count):
        return start + lax.iota(jnp.int32, count)[:, None] == lax.iota(jnp.int32, D)[None, :]

    trace_part = jnp.sum(jnp.where(diag_mask(dp_index * rows, rows), cov_rows, 0.0))
    parts = jnp.stack([trace_part, jnp.sum(cov_rows * cov_rows)])
    grad_rows, sums = ring_reduce(grad_part, 1, ((chips - 3, lambda unused: sum_dp(parts)),))
    grad_rows = grad_rows.astype(bf16)
    if c == 2:
        first = lax.ppermute(grad_rows, "grp", [(0, 1)])
        grad_rows = jnp.concatenate([first, grad_rows], axis=0)
    else:
        grad_rows = lax.all_gather(grad_rows, "grp", axis=0, tiled=True)
    trace, square = sums
    damp = damping * trace / D
    scale = lax.rsqrt(square + 2.0 * damp * trace + D * damp * damp)

    left = series(grad_rows.astype(f32), cov, scale, damp).astype(bf16)
    blocks = left.reshape(rows, n, rows).transpose(1, 0, 2)
    got = []
    for turn in range(n):
        piece = lax.dynamic_index_in_dim(blocks, (dp_index + turn) % n, 0, keepdims=False)
        moves = [
            (i * c + part + j, (i + turn) % n * c + j) for i in range(n) for j in range(part)
        ]
        got.append(lax.ppermute(piece, ("dp", "grp"), moves))
    left = lax.dynamic_slice_in_dim(jnp.stack(2 * got[::-1]), n - 1 - dp_index, n, 0)
    left = left.reshape(chips, 2, c, D // c // n, rows).transpose(2, 1, 0, 3, 4).reshape(D, rows)
    precond = series(left.T.astype(f32), cov, scale, damp)

    total = sum_dp(jnp.sum(precond * precond))

    keep = lax.dynamic_slice_in_dim(precond, (grp_index % part) * cols, cols, 1)
    send = lax.dynamic_slice_in_dim(precond, (grp_index % part + part) * cols, cols, 1)
    sent = lax.ppermute(send.astype(bf16), "grp", [(j, part + j) for j in range(part)])
    precond = jnp.where(on_g, sent.astype(f32), keep)
    total = lax.ppermute(total, "grp", [(j, part + j) for j in range(part)]) + jnp.where(
        on_g, 0.0, total
    )
    return precond * lax.rsqrt(total / (D * D) + epsilon)


def solution(mesh):
    spec = P("dp", "grp")
    return jax.shard_map(shards, mesh=mesh, in_specs=(spec, spec), out_specs=spec, check_vma=False)
```
